1024 devices in a mesh: energy: 64 (over x, y, core), domain: 16 (over z).
Axes of the slice: x: 4, y: 8, z: 16, core: 2. Of those that a mesh axis runs over, the one named last changes fastest.
Arguments:
- hamilton: float32 [16, 256, 256], P('domain'), may hold values from -0.04 to 1.56, as said below
- coupling: float32 [16, 256, 256], P('domain'), may hold values from -0.6 to 0
- left_contact: float32 [64, 256, 256], P('energy'), may hold values from -0.5 to 3, as said below
- right_contact: float32 [64, 256, 256], P('energy'), may hold values from -0.3 to 1.8, as said below
- shifts: float32 [64], P('energy'), may hold values from 0.001 to 0.016
- coulomb: float32 [16, 256, 256], P('domain', 'energy'), may hold values from 0.08 to 0.32
Outputs:
- self_energy: bfloat16 [64, 16, 256, 256], P('energy', 'domain')
The draws below stay inside these ranges and needn't reach their ends.
Inputs may be any that keep to these rules, and one draw needn't show every extreme that they name: `hamilton`: each block is symmetric. `left_contact`: each block is symmetric. `right_contact`: each block is symmetric.
All inputs are finite; a program needn't handle non-finite values.
Results may differ from the reference program's by a relative error of at most 0.0035.
Values may be sent and summed in bfloat16 or wider, within the bound.
A program may use at most 64 MiB of HBM per device.

```python
import math
import jax
import jax.numpy as jnp
from jax import lax

ORB = 256
NB = 16
NE = 64


grid_stride = 16


def link_masks():
    index = jnp.arange(ORB, dtype=jnp.int32)
    near_mask = (index < ORB - 1).astype(jnp.float32)
    far_mask = (index < ORB - grid_stride).astype(jnp.float32)
    return (near_mask, far_mask)


def lift(vector, offset):
    return jnp.pad(vector[:, :ORB - offset], ((0, 0), (offset, 0)))


def lattice(key, count, lowest, highest):
    near_mask, far_mask = link_masks()
    key_near, key_far = jax.random.split(key)
    near = jax.random.uniform(key_near, (count, ORB), jnp.float32, lowest, highest) * near_mask
    far = jax.random.uniform(key_far, (count, ORB), jnp.float32, lowest, highest) * far_mask
    step_one = near[:, :, None] * jnp.eye(ORB, k=1, dtype=jnp.float32)[None]
    step_far = far[:, :, None] * jnp.eye(ORB, k=grid_stride, dtype=jnp.float32)[None]
    upper = step_one + step_far
    hopping = -(upper + jnp.swapaxes(upper, 1, 2))
    weight = near + lift(near, 1) + far + lift(far, grid_stride)
    return (hopping, weight)


def chain_links(key):
    key = jax.random.fold_in(key, 5)
    near_mask, far_mask = link_masks()
    keys = jax.random.split(key, 5)
    along = jax.random.uniform(keys[0], (NB, ORB), jnp.float32, 0.35, 0.6)
    forward_one = jax.random.uniform(keys[1], (NB, ORB), jnp.float32, 0.01, 0.025) * near_mask
    backward_one = jax.random.uniform(keys[2], (NB, ORB), jnp.float32, 0.01, 0.025) * near_mask
    forward_far = jax.random.uniform(keys[3], (NB, ORB), jnp.float32, 0.01, 0.025) * far_mask
    backward_far = jax.random.uniform(keys[4], (NB, ORB), jnp.float32, 0.01, 0.025) * far_mask
    eye_one = jnp.eye(ORB, k=1, dtype=jnp.float32)[None]
    eye_far = jnp.eye(ORB, k=grid_stride, dtype=jnp.float32)[None]
    links = jnp.eye(ORB, dtype=jnp.float32)[None] * along[:, :, None]
    links = links + forward_one[:, :, None] * eye_one
    links = links + jnp.swapaxes(backward_one[:, :, None] * eye_one, 1, 2)
    links = links + forward_far[:, :, None] * eye_far
    links = links + jnp.swapaxes(backward_far[:, :, None] * eye_far, 1, 2)
    row_weight = along + forward_one + lift(backward_one, 1) + forward_far + lift(backward_far, grid_stride)
    column_weight = along + lift(forward_one, 1) + backward_one + lift(forward_far, grid_stride) + backward_far
    return (-links, row_weight, column_weight)


def contact_blocks(key, count, lowest, highest, floor_level, top_level):
    key_hop, key_level = jax.random.split(key)
    hopping, weight = lattice(key_hop, count, lowest, highest)
    level = weight + jax.random.uniform(key_level, (count, ORB), jnp.float32, floor_level, top_level)
    return hopping + jnp.eye(ORB, dtype=jnp.float32)[None] * level[:, None, :]


def draw_hamilton(key, part):
    links, row_weight, column_weight = chain_links(key)
    key = jax.random.fold_in(key, 11)
    hopping, weight = lattice(key, NB, 0.02, 0.04)
    level = weight + column_weight + jnp.roll(row_weight, -1, axis=0)
    return hopping + jnp.eye(ORB, dtype=jnp.float32)[None] * level[:, None, :]


def draw_coupling(key, part):
    links, row_weight, column_weight = chain_links(key)
    return links


def draw_left_contact(key, part):
    key = jax.random.fold_in(key, 23)
    return contact_blocks(key, NE, 0.2, 0.5, 0.3, 1.0)


def draw_right_contact(key, part):
    key = jax.random.fold_in(key, 37)
    return contact_blocks(key, NE, 0.1, 0.3, 0.2, 0.6)


def block_scale(key, extent, cuts, least, largest):
    gain, own = 1.0, jax.random.fold_in(key, 6)
    for axis_at, parts in cuts:
        draws = jnp.exp(jax.random.uniform(jax.random.fold_in(own, axis_at), (parts,), jnp.float32, least / len(cuts), largest / len(cuts)))
        gain = gain * jnp.repeat(draws, extent[axis_at] // parts).reshape([-1 if axis == axis_at else 1 for axis in range(len(extent))])
    return gain


def setup_inputs(seed: int = 0) -> dict:
    streams_of = jax.random.split(jax.random.key(seed), 7)
    return {
        "hamilton": draw_hamilton(jax.random.fold_in(streams_of[6], 71), 0),
        "coupling": draw_coupling(jax.random.fold_in(streams_of[6], 71), 0),
        "left_contact": draw_left_contact(jax.random.fold_in(streams_of[6], 71), 0),
        "right_contact": draw_right_contact(jax.random.fold_in(streams_of[6], 71), 0),
        "shifts": jnp.clip(jnp.exp(math.log(0.016) - 2.7725887 * jax.random.uniform(streams_of[4], (NE,), jnp.float32) ** block_scale(streams_of[4], (NE,), ((0, 64),), -0.2, 0.2)), 0.001, 0.016),
        "coulomb": jnp.clip(jnp.exp(math.log(0.32) - 1.3862944 * jax.random.uniform(streams_of[5], (NB, ORB, ORB), jnp.float32) ** block_scale(streams_of[5], (NB, ORB, ORB), ((0, 16), (1, 64)), -0.2, 0.2)), 0.08, 0.32),
    }


def matmul_hi(left, right):
    return jnp.matmul(left, right, precision=lax.Precision.HIGHEST)

def flip(matrix):
    return jnp.swapaxes(matrix, -1, -2)

def spd_inverse(matrix):
    factor = jnp.linalg.cholesky(matrix)
    unit_matrix = jnp.broadcast_to(jnp.eye(matrix.shape[-1], dtype=matrix.dtype), matrix.shape)
    return jax.scipy.linalg.cho_solve((factor, True), unit_matrix)

def reference(hamilton, coupling, left_contact, right_contact, shifts, coulomb):

    def one_energy(operands):
        shift, left_part, right_part = operands
        unit_matrix = jnp.eye(ORB, dtype=hamilton.dtype)
        chain = hamilton + shift * unit_matrix
        first_link = coupling[0]
        chain = chain.at[0].add(matmul_hi(matmul_hi(flip(first_link), left_part), first_link))
        chain = chain.at[NB - 1].add(right_part)
        start = spd_inverse(chain[0])

        def forward(carry, pair):
            block, link = pair
            following = spd_inverse(block - matmul_hi(matmul_hi(flip(link), carry), link))
            return (following, following)
        _, rest = lax.scan(forward, start, (chain[1:], coupling[1:]))
        left_green = jnp.concatenate([start[None], rest], axis=0)

        def backward(carry, pair):
            local, link = pair
            outer = matmul_hi(local, link)
            value = local + matmul_hi(matmul_hi(outer, carry), flip(outer))
            return (value, value)
        _, earlier = lax.scan(backward, left_green[NB - 1], (left_green[:NB - 1], coupling[1:]), reverse=True)
        return jnp.concatenate([earlier, left_green[NB - 1][None]], axis=0).astype(jnp.bfloat16)
    green = lax.map(one_energy, (shifts, left_contact, right_contact))

    def one_block(operands):
        green_block, strength = operands
        values = green_block.astype(jnp.float32)
        spectrum = jnp.fft.fft(values, n=2 * NE, axis=0)
        polarization = jnp.real(jnp.fft.ifft(spectrum * jnp.conj(spectrum), axis=0))[:NE]
        screened = strength * strength * polarization
        product = spectrum * jnp.fft.fft(screened, n=2 * NE, axis=0)
        total = jnp.real(jnp.fft.ifft(product, axis=0))[:NE]
        return total.astype(jnp.bfloat16)
    result = lax.map(one_block, (jnp.swapaxes(green, 0, 1), coulomb))
    return jnp.swapaxes(result, 0, 1)
```

```python
import functools

import jax
import jax.numpy as jnp
from jax import lax
from jax.experimental import pallas as pl
from jax.experimental.pallas import tpu as pltpu
from jax.sharding import PartitionSpec as P

ORB = 256
HALF = ORB // 2
ROWS = 8
HIGHEST = lax.Precision.HIGHEST
VMEM = pl.BlockSpec(memory_space=pltpu.VMEM)
SMEM = pl.BlockSpec(memory_space=pltpu.SMEM)
PACKED = ORB + ROWS


def dot(left, right, left_dim=1, right_dim=0):
    return lax.dot_general(
        left, right, (((left_dim,), (right_dim,)), ((), ())),
        precision=HIGHEST, preferred_element_type=jnp.float32,
    )


def eliminated_panel(rows, first):
    width = rows.shape[1]
    lane = lax.broadcasted_iota(jnp.int32, rows.shape, 1)
    sublane = lax.broadcasted_iota(jnp.int32, rows.shape, 0)
    spread = [jnp.broadcast_to(rows[:, first + j:first + j + 1], (ROWS, width)) for j in range(ROWS)]
    for k in range(ROWS):
        factor = spread[k]
        scale = 1.0 / factor[k:k + 1, :]
        is_pivot = sublane == k
        for j in range(k + 1, ROWS):
            scaled = spread[j][k:k + 1, :] * scale
            spread[j] = jnp.where(is_pivot, scaled, spread[j] - factor * scaled)
        own_column = lane == first + k
        pivot_row = jnp.where(own_column[:1], 1.0, rows[k:k + 1, :]) * scale
        rows = jnp.where(is_pivot, pivot_row, jnp.where(own_column, 0.0, rows) - factor * pivot_row)
    return rows


def inverse_half(matrix):
    size = matrix.shape[0]
    count = size // ROWS
    lane = lax.broadcasted_iota(jnp.int32, (ROWS, size), 1)
    groups = [matrix[ROWS * i:ROWS * i + ROWS, :] for i in range(count)]
    for t in range(count):
        first = ROWS * t
        pivots = eliminated_panel(groups[t], first)
        groups[t] = pivots
        own = (lane >= first) & (lane < first + ROWS)
        for i in [(t + 1 + i) % count for i in range(count - 1)]:
            rows = groups[i]
            update = rows[:, first:first + 1] * pivots[0:1, :]
            for j in range(1, ROWS):
                update = update + rows[:, first + j:first + j + 1] * pivots[j:j + 1, :]
            groups[i] = jnp.where(own, 0.0, rows) - update
    return jnp.concatenate(groups, axis=0)


def half_indices():
    row = lax.broadcasted_iota(jnp.int32, (HALF, HALF), 0)
    column = lax.broadcasted_iota(jnp.int32, (HALF, HALF), 1)
    return row, column


def pack(matrix, out):
    row, column = half_indices()
    low = matrix[HALF:, HALF:]
    out[:HALF] = matrix[:HALF, HALF:]
    out[HALF:ORB] = jnp.where(row <= column, matrix[:HALF, :HALF], low)
    diagonal = jnp.sum(jnp.where(row == column, low, 0.0), axis=0, keepdims=True)
    out[ORB:] = jnp.broadcast_to(diagonal, (ROWS, HALF))


def unpack(packed):
    row, column = half_indices()
    corner = packed[:HALF]
    both = packed[HALF:ORB]
    turned = both.T
    top = jnp.where(row <= column, both, turned)
    low = jnp.where(row > column, both, turned)
    low = jnp.where(row == column, packed[ORB:ORB + 1], low)
    return jnp.concatenate(
        [jnp.concatenate([top, corner], axis=1), jnp.concatenate([corner.T, low], axis=1)], axis=0
    )


def message(source, target, send, recv, to, axis="domain"):
    return pltpu.make_async_remote_copy(
        src_ref=source, dst_ref=target, send_sem=send, recv_sem=recv,
        device_id={axis: to}, device_id_type=pl.DeviceIdType.MESH,
    )


CHUNKS = ((0, 64), (64, 64), (128, 64), (192, 72))


def chain_kernel(
    shift, hamilton, coupling, left_contact, right_contact, coulomb, out,
    block, matrix, inverse, part, part_inverse, solved, lead, side,
    ups, downs, links, toward, away, longer, across,
    to_ring, from_ring, to_pair, from_pair, to_middle, middle, settled, opposite,
    green, padded, screened, result, arrived,
    load_sem, send_sem, recv_sem, pair_sem, near_sem, far_sem, spread_sem,
):
    place = lax.axis_index("domain")
    count = lax.axis_size("domain")
    me = lax.axis_index("energy")
    energies = green.shape[0]
    quarter = place // 4
    inner = (place >= 4) & (place < 12)
    odd = lax.rem(quarter, 2)
    even = odd == 0
    pair, near, far = place + 4 - 8 * odd, place + 12 - 8 * quarter, lax.rem(place + 8, count)
    loads = [
        pltpu.make_async_copy(source.at[0], target, load_sem.at[i])
        for i, (source, target) in enumerate(
            ((hamilton, block), (coupling, ups.at[0]), (left_contact, lead), (right_contact, side))
        )
    ]
    for load in loads:
        load.start()

    def neighbour(by):
        return lax.rem(place + by + count, count)

    def other(k):
        return lax.rem(me + k, energies)

    peers = [neighbour(1), neighbour(-1), neighbour(2), neighbour(-2), pair, near, far]
    barrier = pltpu.get_barrier_semaphore()
    for peer in peers:
        pl.semaphore_signal(barrier, inc=1, device_id={"domain": peer}, device_id_type=pl.DeviceIdType.MESH)

    def greet(k, carry):
        pl.semaphore_signal(barrier, inc=1, device_id={"energy": other(k)}, device_id_type=pl.DeviceIdType.MESH)
        return carry

    lax.fori_loop(1, energies, greet, 0)
    first_link = message(coupling.at[0], downs.at[0], send_sem.at[0], recv_sem.at[0], neighbour(-1))

    def ring_messages(turn):
        stride = turn + 1
        left, right = neighbour(-stride), neighbour(stride)
        base = 1 + 4 * turn
        return [
            message(to_ring.at[turn, 0], from_ring.at[turn, 0], send_sem.at[base], recv_sem.at[base], left),
            message(to_ring.at[turn, 1], from_ring.at[turn, 1], send_sem.at[base + 1], recv_sem.at[base + 1], right),
            message(links.at[turn], downs.at[turn + 1], send_sem.at[base + 2], recv_sem.at[base + 2], left),
            message(links.at[turn], ups.at[turn + 1], send_sem.at[base + 3], recv_sem.at[base + 3], right),
        ]

    def chunk_messages(source, target, send, recv, to):
        return [
            message(source.at[pl.ds(*rows)], target.at[pl.ds(*rows)], send.at[i], recv.at[i], to)
            for i, rows in enumerate(CHUNKS)
        ]

    pair_messages = chunk_messages(to_pair, from_pair, pair_sem.at[0], pair_sem.at[1], pair)
    near_messages = chunk_messages(settled, opposite, near_sem.at[0], near_sem.at[1], near)
    far_messages = chunk_messages(settled, opposite, far_sem.at[0], near_sem.at[1], far)
    middle_message = message(to_middle, middle, send_sem.at[9], recv_sem.at[9], pair)
    link_message = message(longer, across, send_sem.at[10], recv_sem.at[10], pair)

    def before_first():
        for load in loads:
            load.wait()
        row = lax.broadcasted_iota(jnp.int32, (ORB, ORB), 0)
        column = lax.broadcasted_iota(jnp.int32, (ORB, ORB), 1)
        block[...] += jnp.where(row == column, shift[0], 0.0)

        @pl.when(place == 0)
        def _():
            link = ups[0]
            block[...] += dot(link, dot(lead[...], link), 0, 0)
            ups[0] = jnp.zeros((ORB, ORB), jnp.float32)

        @pl.when(place == count - 1)
        def _():
            block[...] += side[...]

        matrix[...] = block[...]

    def before_ring(turn):
        messages = ring_messages(turn)
        messages[0].wait_recv()
        messages[1].wait_recv()

        @pl.when(turn == 0)
        def _():
            left_inverse = unpack(from_ring[turn, 1])
            block[...] -= dot(ups[0], dot(left_inverse, ups[0]), 0, 0)

        @pl.when(turn == 1)
        def _():
            block[...] -= unpack(from_ring[turn, 1])

        block[...] -= unpack(from_ring[turn, 0])
        matrix[...] = block[...]

    def before_middle():
        @pl.when(inner)
        def _():
            pack(block[...], settled)
            for i, rows in enumerate(CHUNKS):
                pair_messages[i].wait_recv()
                settled[pl.ds(*rows)] -= from_pair[pl.ds(*rows)]
                far_messages[i].start()
                near_messages[i].start()
            block[...] = unpack(settled[...])
            for received in near_messages:
                received.wait_recv()
            matrix[...] = unpack(opposite[...])

        @pl.when(jnp.logical_not(inner))
        def _():
            for received in pair_messages:
                received.wait_recv()
            block[...] -= unpack(from_pair[...])
            middle_message.wait_recv()
            for received in far_messages:
                received.wait_recv()
            matrix[...] = unpack(opposite[...] - middle[...])

    def before_last():
        @pl.when(inner)
        def _():
            across[...] = away[...].T

        @pl.when(jnp.logical_not(inner))
        def _():
            link_message.wait_recv()

        link = across[...]
        block[...] -= dot(link, dot(inverse[...], link), 0, 0)
        matrix[...] = block[...]

    def after_ring(turn):
        messages = ring_messages(turn)

        @pl.when(turn == 0)
        def _():
            pack(inverse[...], to_ring.at[turn, 1])
            messages[1].start()

        @pl.when(turn == 1)
        def _():
            for received in ring_messages(0)[2:]:
                received.wait_recv()

        pack(dot(ups[turn], dot(inverse[...], ups[turn], 1, 1)), to_ring.at[turn, 0])
        messages[0].start()

        @pl.when(turn == 0)
        def _():
            first_link.wait_recv()

            @pl.when(place == count - 1)
            def _():
                downs[0] = jnp.zeros((ORB, ORB), jnp.float32)

        matrix[...] = dot(inverse[...], downs[turn])

        @pl.when(turn == 1)
        def _():
            pack(dot(downs[turn], matrix[...], 0, 0), to_ring.at[turn, 1])
            messages[1].start()

        links[turn] = -dot(ups[turn], matrix[...])
        messages[2].start()
        messages[3].start()

    def after_pair():
        for received in ring_messages(1)[2:]:
            received.wait_recv()
        turned = ups[2].T
        toward[...] = jnp.where(even, downs[2], turned)
        pack(dot(toward[...], dot(inverse[...], toward[...]), 0, 0), to_pair)
        for sent in pair_messages:
            sent.start()
        away[...] = jnp.where(even, turned, downs[2])

        @pl.when(inner)
        def _():
            matrix[...] = dot(inverse[...], away[...])
            pack(dot(away[...], matrix[...], 0, 0), to_middle)
            middle_message.start()
            longer[...] = -dot(matrix[...], toward[...], 0, 0)
            link_message.start()

    def turn_half(step, carry):
        turn, half = step // 2, lax.rem(step, 2)

        @pl.when(step == 1)
        def _():
            pl.semaphore_wait(barrier, len(peers) + energies - 1)
            first_link.start()

        @pl.when(half == 0)
        def _():
            pl.when(turn == 0)(before_first)
            pl.when((turn == 1) | (turn == 2))(lambda: before_ring(turn - 1))
            pl.when(turn == 3)(before_middle)
            pl.when(turn == 4)(before_last)
            part[...] = matrix[:HALF, :HALF]

        @pl.when(half == 1)
        def _():
            top = part_inverse[...]
            corner = matrix[:HALF, HALF:]
            inverse[:HALF, :HALF] = top
            solved[...] = dot(top, corner)
            part[...] = matrix[HALF:, HALF:] - dot(corner, solved[...], 0, 0)

        part_inverse[...] = inverse_half(part[...])

        @pl.when(half == 1)
        def _():
            low = part_inverse[...]
            corner = dot(solved[...], low)
            inverse[:HALF, :HALF] += dot(corner, solved[...], 1, 1)
            inverse[:HALF, HALF:] = -corner
            inverse[HALF:, :HALF] = -corner.T
            inverse[HALF:, HALF:] = low
            pl.when(turn <= 1)(lambda: after_ring(turn))
            pl.when(turn == 2)(after_pair)

        return carry

    lax.fori_loop(0, 10, turn_half, 0)
    for e in range(energies):
        rows = inverse[4 * e:4 * e + 4, :]
        tile = jnp.concatenate([rows[:, :HALF], rows[:, HALF:]], axis=0)
        green[e] = tile.astype(jnp.bfloat16).astype(jnp.float32)

    def exchange(source, target, offset, index):
        own = pltpu.make_async_copy(source.at[me], target.at[offset + me], load_sem.at[4 + index])
        own.start()

        def send(k, carry):
            to = other(k)
            message(
                source.at[to], target.at[offset + me], spread_sem.at[0, index], spread_sem.at[1, index], to, "energy",
            ).start()
            return carry

        lax.fori_loop(1, energies, send, 0)
        return own, message(
            source.at[pl.ds(0, energies - 1)], target.at[pl.ds(offset, energies - 1)],
            spread_sem.at[0, index], spread_sem.at[1, index], other(1), "energy",
        )

    own, rest = exchange(green, padded, 8, 0)
    padded[:8] = jnp.zeros((8, ROWS, HALF), jnp.float32)
    padded[8 + energies:] = jnp.zeros((8, ROWS, HALF), jnp.float32)
    factor = jnp.concatenate([coulomb[0, :, :HALF], coulomb[0, :, HALF:]], axis=0)
    factor = factor * factor
    first_link.wait_send()
    for turn in range(2):
        for sent in ring_messages(turn):
            sent.wait_send()
    for sent in pair_messages:
        sent.wait_send()

    @pl.when(inner)
    def _():
        for sent in (middle_message, link_message, *near_messages, *far_messages):
            sent.wait_send()

    own.wait()
    rest.wait()
    blocks = energies // 8
    for kb in range(blocks):
        sums = [None] * 8
        for jb in range(blocks - kb):
            base = [padded[8 + 8 * jb + a] for a in range(8)]
            ahead = [padded[8 + 8 * (jb + kb) + c] for c in range(15)]
            for b in range(8):
                for a in range(8):
                    term = base[a] * ahead[a + b]
                    sums[b] = term if sums[b] is None else sums[b] + term
        for b in range(8):
            screened[8 * kb + b] = factor * sums[b]
    for kb in range(blocks):
        sums = [None] * 8
        for jb in range(kb + 1):
            base = [screened[8 * jb + a] for a in range(8)]
            behind = [padded[8 + 8 * (kb - jb) + c - 7] for c in range(15)]
            for b in range(8):
                for a in range(8):
                    term = base[a] * behind[b - a + 7]
                    sums[b] = term if sums[b] is None else sums[b] + term
        for b in range(8):
            result[8 * kb + b] = sums[b]
    own, rest = exchange(result, arrived, 0, 1)
    own.wait()
    rest.wait()
    for q in range(energies // 4):
        rows = [
            jnp.concatenate([arrived[4 * q + t, :4, :], arrived[4 * q + t, 4:, :]], axis=1) for t in range(4)
        ]
        out[16 * q:16 * q + 16, :] = jnp.concatenate(rows, axis=0).astype(jnp.bfloat16)


TILES = (ORB // 4, ROWS, HALF)


def on_device(hamilton, coupling, left_contact, right_contact, shifts, coulomb):
    def several(*shape):
        return pltpu.VMEM(shape, jnp.float32)

    square = several(ORB, ORB)
    half = several(HALF, HALF)
    packed = several(PACKED, HALF)
    tiles = several(*TILES)
    chunked = pltpu.SemaphoreType.DMA((2, len(CHUNKS)))
    result = pl.pallas_call(
        chain_kernel,
        out_shape=jax.ShapeDtypeStruct((ORB, ORB), jnp.bfloat16),
        in_specs=[SMEM] + [pl.BlockSpec(memory_space=pl.ANY)] * 4 + [VMEM],
        out_specs=VMEM,
        scratch_shapes=[
            square, square, square, half, half, half, square, square,
            several(3, ORB, ORB), several(3, ORB, ORB), several(2, ORB, ORB), square, square, square, square,
            several(2, 2, PACKED, HALF), several(2, 2, PACKED, HALF),
            packed, packed, packed, packed, packed, packed,
            tiles, several(TILES[0] + 16, ROWS, HALF), tiles, tiles, tiles,
            pltpu.SemaphoreType.DMA((6,)), pltpu.SemaphoreType.DMA((11,)), pltpu.SemaphoreType.DMA((11,)),
            chunked, chunked, chunked, pltpu.SemaphoreType.DMA((2, 2)),
        ],
        compiler_params=pltpu.CompilerParams(
            vmem_limit_bytes=56 * 1024 * 1024, collective_id=0, has_side_effects=True,
        ),
    )(shifts, hamilton, coupling, left_contact, right_contact, coulomb)
    return result[None, None]


def solution(mesh):
    placed = (
        P("domain", None, None),
        P("domain", None, None),
        P("energy", None, None),
        P("energy", None, None),
        P("energy"),
        P("domain", "energy", None),
    )
    return jax.shard_map(
        on_device,
        mesh=mesh,
        in_specs=placed,
        out_specs=P("energy", "domain", None, None),
        check_vma=False,
    )
```

```python
import functools

import jax
import jax.numpy as jnp
from jax import lax
from jax.experimental import pallas as pl
from jax.experimental.pallas import tpu as pltpu
from jax.sharding import PartitionSpec as P

ORB = 256
HALF = ORB // 2
ROWS = 8
HIGHEST = lax.Precision.HIGHEST
VMEM = pl.BlockSpec(memory_space=pltpu.VMEM)
SMEM = pl.BlockSpec(memory_space=pltpu.SMEM)
PACKED = ORB + ROWS


def dot(left, right, left_dim=1, right_dim=0):
    return lax.dot_general(
        left, right, (((left_dim,), (right_dim,)), ((), ())),
        precision=HIGHEST, preferred_element_type=jnp.float32,
    )


def pivot_steps(rows, first, done):
    width = rows.shape[1]
    lane = lax.broadcasted_iota(jnp.int32, rows.shape, 1)
    sublane = lax.broadcasted_iota(jnp.int32, rows.shape, 0)
    spread = [jnp.broadcast_to(rows[:, first + j:first + j + 1], (ROWS, width)) for j in range(ROWS)]
    yield
    for k in range(0, ROWS, 2):
        left, right = spread[k], spread[k + 1]
        a00, a10 = left[k:k + 1, :], left[k + 1:k + 2, :]
        a01, a11 = right[k:k + 1, :], right[k + 1:k + 2, :]
        scale = 1.0 / (a00 * a11 - a01 * a10)
        is_first, is_second = sublane == k, sublane == k + 1

        def eliminated(x0, x1, rest):
            y0 = (a11 * x0 - a01 * x1) * scale
            y1 = (a00 * x1 - a10 * x0) * scale
            return jnp.where(is_first, y0, jnp.where(is_second, y1, rest - (left * y0 + right * y1)))

        for j in range(k + 2, ROWS):
            spread[j] = eliminated(spread[j][k:k + 1, :], spread[j][k + 1:k + 2, :], spread[j])
        own0, own1 = lane == first + k, lane == first + k + 1
        x0 = jnp.where(own0[:1], 1.0, jnp.where(own1[:1], 0.0, rows[k:k + 1, :]))
        x1 = jnp.where(own1[:1], 1.0, jnp.where(own0[:1], 0.0, rows[k + 1:k + 2, :]))
        rows = eliminated(x0, x1, jnp.where(own0 | own1, 0.0, rows))
        yield
    done.append(rows)


LAZY = 8


def inverse_half(matrix):
    size = matrix.shape[0]
    count = size // ROWS
    lane = lax.broadcasted_iota(jnp.int32, (ROWS, size), 1)
    groups = [matrix[ROWS * i:ROWS * i + ROWS, :] for i in range(count)]

    def update(i, t, pivots, own):
        rows = groups[i]
        change = rows[:, ROWS * t:ROWS * t + 1] * pivots[0:1, :]
        for j in range(1, ROWS):
            change = change + rows[:, ROWS * t + j:ROWS * t + j + 1] * pivots[j:j + 1, :]
        groups[i] = jnp.where(own, 0.0, rows) - change

    done = []
    for _ in pivot_steps(groups[0], 0, done):
        pass
    groups[0] = done[0]
    for t in range(count):
        pivots = groups[t]
        own = (lane >= ROWS * t) & (lane < ROWS * t + ROWS)
        waiting = list(range(t + 2, count)) + list(range(LAZY * (t // LAZY), t))
        if t + 1 < count:
            update(t + 1, t, pivots, own)
            done = []
            share = -(-len(waiting) // (ROWS // 2 + 1))
            for _ in pivot_steps(groups[t + 1], ROWS * (t + 1), done):
                for i in waiting[:share]:
                    update(i, t, pivots, own)
                waiting = waiting[share:]
            groups[t + 1] = done[0]
        for i in waiting:
            update(i, t, pivots, own)
        if t % LAZY == LAZY - 1 and t >= LAZY:
            start = LAZY * (t // LAZY)
            before = jnp.concatenate(groups[:start], axis=0)
            run = jnp.concatenate(groups[start:start + LAZY], axis=0)
            low, high = ROWS * start, ROWS * (start + LAZY)
            columns = lax.broadcasted_iota(jnp.int32, before.shape, 1)
            kept = jnp.where((columns >= low) & (columns < high), 0.0, before)
            before = kept - dot(before[:, low:high], run)
            for i in range(start):
                groups[i] = before[ROWS * i:ROWS * i + ROWS]
    return jnp.concatenate(groups, axis=0)


def half_indices():
    row = lax.broadcasted_iota(jnp.int32, (HALF, HALF), 0)
    column = lax.broadcasted_iota(jnp.int32, (HALF, HALF), 1)
    return row, column


def pack(matrix, out):
    row, column = half_indices()
    low = matrix[HALF:, HALF:]
    out[:HALF] = matrix[:HALF, HALF:]
    out[HALF:ORB] = jnp.where(row <= column, matrix[:HALF, :HALF], low)
    diagonal = jnp.sum(jnp.where(row == column, low, 0.0), axis=0, keepdims=True)
    out[ORB:] = jnp.broadcast_to(diagonal, (ROWS, HALF))


def unpack_ends(both, diagonal):
    row, column = half_indices()
    turned = both.T
    top = jnp.where(row <= column, both, turned)
    low = jnp.where(row > column, both, turned)
    return top, jnp.where(row == column, diagonal, low)


def unpack(packed):
    corner = packed[:HALF]
    top, low = unpack_ends(packed[HALF:ORB], packed[ORB:ORB + 1])
    return jnp.concatenate(
        [jnp.concatenate([top, corner], axis=1), jnp.concatenate([corner.T, low], axis=1)], axis=0
    )


def message(source, target, send, recv, to, axis="domain"):
    return pltpu.make_async_remote_copy(
        src_ref=source, dst_ref=target, send_sem=send, recv_sem=recv,
        device_id={axis: to}, device_id_type=pl.DeviceIdType.MESH,
    )


def energy_peers():
    me = lax.axis_index("energy")
    count = lax.axis_size("energy")
    core = lax.rem(me, 2)
    return me + 1 - 2 * core, lambda k: lax.rem(me + 2 * k, count)


def energy_part(
    inverse, coulomb, out, green, landed, parity, to_twin, sums_of, from_twin, returned, final,
    own_sem, spread_sem, twin_sem,
):
    me = lax.axis_index("energy")
    chip, core = me // 2, lax.rem(me, 2)
    chips = green.shape[0]
    twin, other = energy_peers()
    first_core = core == 0

    def exchange(source, target, index):
        own = pltpu.make_async_copy(source.at[chip], target.at[chip], own_sem.at[index])
        own.start()

        def send(k, carry):
            to = other(k)
            message(
                source.at[to // 2], target.at[chip], spread_sem.at[0, index], spread_sem.at[1, index], to, "energy",
            ).start()
            return carry

        lax.fori_loop(1, chips, send, 0)
        return own, message(
            source.at[pl.ds(0, chips - 1)], target.at[pl.ds(0, chips - 1)],
            spread_sem.at[0, index], spread_sem.at[1, index], other(1), "energy",
        )

    for t in range(chips):
        rows = inverse[ROWS * t:ROWS * t + ROWS, :]
        green[t] = jnp.concatenate([rows[:, :HALF], rows[:, HALF:]], axis=0).astype(jnp.bfloat16)
    own, rest = exchange(green, landed, 0)
    pad = jnp.zeros((2, 4, ROWS, HALF), jnp.float32)
    parity[:, :4] = pad
    parity[:, 4 + chips:] = pad
    factor = jnp.concatenate([coulomb[0, :, :HALF], coulomb[0, :, HALF:]], axis=0)
    factor = factor * factor
    own.wait()
    rest.wait()
    for t in range(chips):
        both = landed[t].astype(jnp.float32)
        upper = jnp.concatenate([both[:4], both[8:12]], axis=0)
        lower = jnp.concatenate([both[4:8], both[12:]], axis=0)
        parity[core, 4 + t] = jnp.where(first_core, upper, lower)
        to_twin[t] = jnp.where(first_core, lower, upper)
    swap = message(to_twin, parity.at[core, pl.ds(4, chips)], twin_sem.at[0], twin_sem.at[1], twin, "energy")
    swap.start()
    swap.wait()

    def at(energy):
        return parity[energy % 2, 4 + energy // 2]

    blocks = 2 * chips // 8
    for kb in range(blocks):
        sums = [None] * 8
        for jb in range(blocks - kb):
            base = [at(8 * jb + a) for a in range(8)]
            ahead = [at(8 * (jb + kb) + c) for c in range(15)]
            for b in range(8):
                for a in range(8):
                    term = base[a] * ahead[a + b]
                    sums[b] = term if sums[b] is None else sums[b] + term
        for b in range(8):
            returned[8 * kb + b] = factor * sums[b]
    for kb in range(blocks):
        sums = [None] * 8
        for jb in range(kb + 1):
            base = [returned[8 * jb + a] for a in range(8)]
            behind = [at(8 * (kb - jb) + c - 7) for c in range(15)]
            for b in range(8):
                for a in range(8):
                    term = base[a] * behind[b - a + 7]
                    sums[b] = term if sums[b] is None else sums[b] + term
        for b in range(8):
            sums_of[b % 2, 4 * kb + b // 2] = sums[b]
    swap = message(sums_of.at[1 - core], from_twin, twin_sem.at[2], twin_sem.at[3], twin, "energy")
    swap.start()
    swap.wait()
    for t in range(chips):
        mine, theirs = sums_of[core, t], from_twin[t]
        upper = jnp.where(first_core, mine, theirs)
        lower = jnp.where(first_core, theirs, mine)
        both = jnp.concatenate([upper[:4], lower[:4], upper[4:], lower[4:]], axis=0)
        green[t] = both.astype(jnp.bfloat16)
    own, rest = exchange(green, final, 1)
    own.wait()
    rest.wait()
    out[...] = final[...]


ENERGY_SCRATCH = (
    ((32, 16, HALF), jnp.bfloat16), ((32, 16, HALF), jnp.bfloat16), ((2, 40, ROWS, HALF), jnp.float32),
    ((32, ROWS, HALF), jnp.float32), ((2, 32, ROWS, HALF), jnp.float32), ((32, ROWS, HALF), jnp.float32),
    ((64, ROWS, HALF), jnp.float32), ((32, 16, HALF), jnp.bfloat16),
)


def energy_scratch():
    return [pltpu.VMEM(*buffer) for buffer in ENERGY_SCRATCH] + [
        pltpu.SemaphoreType.DMA((2,)), pltpu.SemaphoreType.DMA((2, 2)), pltpu.SemaphoreType.DMA((4,)),
    ]


CHUNKS = ((128, 64), (192, 72), (0, 64), (64, 64))
ENDS, CORNER = pl.ds(HALF, PACKED - HALF), pl.ds(0, HALF)


def chain_kernel(
    shift, hamilton, coupling, left_contact, right_contact, coulomb, out,
    block, matrix, inverse, part, part_inverse, solved, lead, side,
    ups, downs, links, toward, away, longer, across,
    to_ring, from_ring, to_pair, from_pair, to_middle, middle, settled, distant, opposite,
    load_sem, send_sem, recv_sem, pair_sem, near_sem, far_sem, middle_sem,
    green, landed, parity, to_twin, sums_of, from_twin, returned, final, own_sem, spread_sem, twin_sem,
):
    place = lax.axis_index("domain")
    count = lax.axis_size("domain")
    chips = green.shape[0]
    twin, other = energy_peers()
    quarter = place // 4
    inner = (place >= 4) & (place < 12)
    odd = lax.rem(quarter, 2)
    even = odd == 0
    pair, near, far = place + 4 - 8 * odd, place + 12 - 8 * quarter, lax.rem(place + 8, count)
    loads = [
        pltpu.make_async_copy(source.at[0], target, load_sem.at[i])
        for i, (source, target) in enumerate(
            ((hamilton, block), (coupling, ups.at[0]), (left_contact, lead), (right_contact, side))
        )
    ]
    for load in loads:
        load.start()

    def neighbour(by):
        return lax.rem(place + by + count, count)

    peers = [neighbour(1), neighbour(-1), neighbour(2), neighbour(-2), pair, near, far]
    barrier = pltpu.get_barrier_semaphore()
    for peer in peers:
        pl.semaphore_signal(barrier, inc=1, device_id={"domain": peer}, device_id_type=pl.DeviceIdType.MESH)

    def greet(k, carry):
        pl.semaphore_signal(barrier, inc=1, device_id={"energy": other(k)}, device_id_type=pl.DeviceIdType.MESH)
        return carry

    lax.fori_loop(1, chips, greet, 0)
    pl.semaphore_signal(barrier, inc=1, device_id={"energy": twin}, device_id_type=pl.DeviceIdType.MESH)
    first_link = message(coupling.at[0], downs.at[0], send_sem.at[0], recv_sem.at[0], neighbour(-1))

    def ring_messages(turn):
        stride = turn + 1
        left, right = neighbour(-stride), neighbour(stride)
        base = 1 + 6 * turn
        return [
            message(
                to_ring.at[turn, side_id, rows], from_ring.at[turn, side_id, rows],
                send_sem.at[base + i], recv_sem.at[base + i], to,
            )
            for i, (side_id, rows, to) in enumerate(
                ((0, ENDS, left), (1, ENDS, right), (0, CORNER, left), (1, CORNER, right))
            )
        ] + [
            message(links.at[turn], downs.at[turn + 1], send_sem.at[base + 4], recv_sem.at[base + 4], left),
            message(links.at[turn], ups.at[turn + 1], send_sem.at[base + 5], recv_sem.at[base + 5], right),
        ]

    def chunk_messages(source, target, send, recv, to):
        return [
            message(source.at[pl.ds(*rows)], target.at[pl.ds(*rows)], send.at[i], recv.at[i], to)
            for i, rows in enumerate(CHUNKS)
        ]

    pair_messages = chunk_messages(to_pair, from_pair, pair_sem.at[0], pair_sem.at[1], pair)
    near_messages = chunk_messages(settled, opposite, near_sem.at[0], near_sem.at[1], near)
    far_messages = chunk_messages(distant, opposite, far_sem.at[0], near_sem.at[1], far)
    middle_messages = chunk_messages(to_middle, middle, middle_sem.at[0], middle_sem.at[1], near)
    link_message = message(longer, across, send_sem.at[13], recv_sem.at[13], pair)

    def before_first():
        for load in loads:
            load.wait()
        row = lax.broadcasted_iota(jnp.int32, (ORB, ORB), 0)
        column = lax.broadcasted_iota(jnp.int32, (ORB, ORB), 1)
        block[...] += jnp.where(row == column, shift[0], 0.0)

        @pl.when(place == 0)
        def _():
            link = ups[0]
            block[...] += dot(link, dot(lead[...], link), 0, 0)
            ups[0] = jnp.zeros((ORB, ORB), jnp.float32)

        @pl.when(place == count - 1)
        def _():
            block[...] += side[...]

        matrix[...] = block[...]

    def before_ring(turn):
        messages = ring_messages(turn)
        messages[0].wait_recv()
        messages[1].wait_recv()

        @pl.when(turn == 0)
        def _():
            messages[2].wait_recv()
            messages[3].wait_recv()
            left_inverse = unpack(from_ring[0, 1])
            block[...] -= dot(ups[0], dot(left_inverse, ups[0]), 0, 0)
            block[...] -= unpack(from_ring[0, 0])
            matrix[...] = block[...]

        @pl.when(turn == 1)
        def _():
            ends = from_ring[1, 0, HALF:, :] + from_ring[1, 1, HALF:, :]
            top, low = unpack_ends(ends[:HALF], ends[HALF:HALF + 1])
            block[:HALF, :HALF] -= top
            block[HALF:, HALF:] -= low
            matrix[:HALF, :HALF] = block[:HALF, :HALF]
            matrix[HALF:, HALF:] = block[HALF:, HALF:]

    def before_ring_corner():
        for received in ring_messages(1)[2:4]:
            received.wait_recv()
        corner = block[:HALF, HALF:] - from_ring[1, 0, :HALF, :] - from_ring[1, 1, :HALF, :]
        block[:HALF, HALF:] = corner
        block[HALF:, :HALF] = corner.T
        matrix[:HALF, HALF:] = corner

    def before_middle():
        @pl.when(inner)
        def _():
            pack(block[...], settled)
            for i, rows in enumerate(CHUNKS):
                pair_messages[i].wait_recv()
                settled[pl.ds(*rows)] -= from_pair[pl.ds(*rows)]
                near_messages[i].start()
                middle_messages[i].wait_recv()
                distant[pl.ds(*rows)] = settled[pl.ds(*rows)] - middle[pl.ds(*rows)]
                far_messages[i].start()
            block[...] = unpack(settled[...])
            for received in near_messages[:2]:
                received.wait_recv()

        @pl.when(jnp.logical_not(inner))
        def _():
            for received in pair_messages:
                received.wait_recv()
            block[...] -= unpack(from_pair[...])
            for received in far_messages[:2]:
                received.wait_recv()

        ends = opposite[HALF:, :]
        top, low = unpack_ends(ends[:HALF], ends[HALF:HALF + 1])
        matrix[:HALF, :HALF] = top
        matrix[HALF:, HALF:] = low

    def before_middle_corner():
        for received in near_messages[2:]:
            received.wait_recv()
        matrix[:HALF, HALF:] = opposite[:HALF, :]

    def before_last():
        @pl.when(inner)
        def _():
            across[...] = away[...].T

        @pl.when(jnp.logical_not(inner))
        def _():
            link_message.wait_recv()

        link = across[...]
        block[...] -= dot(link, dot(inverse[...], link), 0, 0)
        matrix[...] = block[...]

    def after_ring(turn):
        messages = ring_messages(turn)

        @pl.when(turn == 0)
        def _():
            pack(inverse[...], to_ring.at[turn, 1])
            messages[1].start()
            messages[3].start()

        @pl.when(turn == 1)
        def _():
            for received in ring_messages(0)[4:]:
                received.wait_recv()

        pack(dot(ups[turn], dot(inverse[...], ups[turn], 1, 1)), to_ring.at[turn, 0])
        messages[0].start()
        messages[2].start()

        @pl.when(turn == 0)
        def _():
            first_link.wait_recv()

            @pl.when(place == count - 1)
            def _():
                downs[0] = jnp.zeros((ORB, ORB), jnp.float32)

        matrix[...] = dot(inverse[...], downs[turn])

        @pl.when(turn == 1)
        def _():
            pack(dot(downs[turn], matrix[...], 0, 0), to_ring.at[turn, 1])
            messages[1].start()
            messages[3].start()

        links[turn] = -dot(ups[turn], matrix[...])
        messages[4].start()
        messages[5].start()

    def after_pair():
        for received in ring_messages(1)[4:]:
            received.wait_recv()
        turned = ups[2].T
        toward[...] = jnp.where(even, downs[2], turned)
        pack(dot(toward[...], dot(inverse[...], toward[...]), 0, 0), to_pair)
        for sent in pair_messages:
            sent.start()
        away[...] = jnp.where(even, turned, downs[2])

        @pl.when(inner)
        def _():
            matrix[...] = dot(inverse[...], away[...])
            pack(dot(away[...], matrix[...], 0, 0), to_middle)
            for sent in middle_messages:
                sent.start()
            longer[...] = -dot(matrix[...], toward[...], 0, 0)
            link_message.start()

    def turn_half(step, carry):
        turn, half = step // 2, lax.rem(step, 2)

        @pl.when(step == 1)
        def _():
            pl.semaphore_wait(barrier, len(peers) + chips)
            first_link.start()

        @pl.when(half == 0)
        def _():
            pl.when(turn == 0)(before_first)
            pl.when((turn == 1) | (turn == 2))(lambda: before_ring(turn - 1))
            pl.when(turn == 3)(before_middle)
            pl.when(turn == 4)(before_last)
            part[...] = matrix[:HALF, :HALF]

        @pl.when(half == 1)
        def _():
            pl.when(turn == 2)(before_ring_corner)
            pl.when(turn == 3)(before_middle_corner)
            top = part_inverse[...]
            corner = matrix[:HALF, HALF:]
            inverse[:HALF, :HALF] = top
            solved[...] = dot(top, corner)
            part[...] = matrix[HALF:, HALF:] - dot(corner, solved[...], 0, 0)

        part_inverse[...] = inverse_half(part[...])

        @pl.when(half == 1)
        def _():
            low = part_inverse[...]
            corner = dot(solved[...], low)
            inverse[:HALF, :HALF] += dot(corner, solved[...], 1, 1)
            inverse[:HALF, HALF:] = -corner
            inverse[HALF:, :HALF] = -corner.T
            inverse[HALF:, HALF:] = low
            pl.when(turn <= 1)(lambda: after_ring(turn))
            pl.when(turn == 2)(after_pair)

        return carry

    lax.fori_loop(0, 10, turn_half, 0)
    energy_part(
        inverse, coulomb, out, green, landed, parity, to_twin, sums_of, from_twin, returned, final,
        own_sem, spread_sem, twin_sem,
    )
    first_link.wait_send()
    for turn in range(2):
        for sent in ring_messages(turn):
            sent.wait_send()
    for sent in pair_messages:
        sent.wait_send()

    @pl.when(inner)
    def _():
        for sent in (link_message, *middle_messages, *near_messages, *far_messages):
            sent.wait_send()


def on_device(hamilton, coupling, left_contact, right_contact, shifts, coulomb):
    def several(*shape):
        return pltpu.VMEM(shape, jnp.float32)

    square = several(ORB, ORB)
    half = several(HALF, HALF)
    packed = several(PACKED, HALF)
    chunked = pltpu.SemaphoreType.DMA((2, len(CHUNKS)))
    result = pl.pallas_call(
        chain_kernel,
        out_shape=jax.ShapeDtypeStruct((ORB // ROWS, 2 * ROWS, HALF), jnp.bfloat16),
        in_specs=[SMEM] + [pl.BlockSpec(memory_space=pl.ANY)] * 4 + [VMEM],
        out_specs=VMEM,
        scratch_shapes=[
            square, square, square, half, half, half, square, square,
            several(3, ORB, ORB), several(3, ORB, ORB), several(2, ORB, ORB), square, square, square, square,
            several(2, 2, PACKED, HALF), several(2, 2, PACKED, HALF),
            packed, packed, packed, packed, packed, packed, packed,
            pltpu.SemaphoreType.DMA((4,)), pltpu.SemaphoreType.DMA((14,)), pltpu.SemaphoreType.DMA((14,)),
            chunked, chunked, chunked, chunked, *energy_scratch(),
        ],
        compiler_params=pltpu.CompilerParams(
            vmem_limit_bytes=56 * 1024 * 1024, collective_id=0, has_side_effects=True,
        ),
    )(shifts, hamilton, coupling, left_contact, right_contact, coulomb)
    result = result.reshape(ORB // ROWS, 2, ROWS, HALF).transpose(0, 2, 1, 3)
    return result.reshape(1, 1, ORB, ORB)


def solution(mesh):
    placed = (
        P("domain", None, None),
        P("domain", None, None),
        P("energy", None, None),
        P("energy", None, None),
        P("energy"),
        P("domain", "energy", None),
    )
    return jax.shard_map(
        on_device,
        mesh=mesh,
        in_specs=placed,
        out_specs=P("energy", "domain", None, None),
        check_vma=False,
    )
```

```python
import functools

import jax
import jax.numpy as jnp
from jax import lax
from jax.experimental import pallas as pl
from jax.experimental.pallas import tpu as pltpu
from jax.sharding import PartitionSpec as P

ORB = 256
HALF = ORB // 2
ROWS = 8
HIGHEST = lax.Precision.HIGHEST
VMEM = pl.BlockSpec(memory_space=pltpu.VMEM)
SMEM = pl.BlockSpec(memory_space=pltpu.SMEM)
PACKED = ORB + ROWS


def dot(left, right, left_dim=1, right_dim=0):
    return lax.dot_general(
        left, right, (((left_dim,), (right_dim,)), ((), ())),
        precision=HIGHEST, preferred_element_type=jnp.float32,
    )


def pivot_steps(rows, first, done):
    width = rows.shape[1]
    lane = lax.broadcasted_iota(jnp.int32, rows.shape, 1)
    sublane = lax.broadcasted_iota(jnp.int32, rows.shape, 0)
    spread = [jnp.broadcast_to(rows[:, first + j:first + j + 1], (ROWS, width)) for j in range(ROWS)]
    yield
    for k in range(0, ROWS, 2):
        left, right = spread[k], spread[k + 1]
        a00, a10 = left[k:k + 1, :], left[k + 1:k + 2, :]
        a01, a11 = right[k:k + 1, :], right[k + 1:k + 2, :]
        scale = 1.0 / (a00 * a11 - a01 * a10)
        is_first, is_second = sublane == k, sublane == k + 1

        def eliminated(x0, x1, rest):
            y0 = (a11 * x0 - a01 * x1) * scale
            y1 = (a00 * x1 - a10 * x0) * scale
            return jnp.where(is_first, y0, jnp.where(is_second, y1, rest - (left * y0 + right * y1)))

        for j in range(k + 2, ROWS):
            spread[j] = eliminated(spread[j][k:k + 1, :], spread[j][k + 1:k + 2, :], spread[j])
        own0, own1 = lane == first + k, lane == first + k + 1
        x0 = jnp.where(own0[:1], 1.0, jnp.where(own1[:1], 0.0, rows[k:k + 1, :]))
        x1 = jnp.where(own1[:1], 1.0, jnp.where(own0[:1], 0.0, rows[k + 1:k + 2, :]))
        rows = eliminated(x0, x1, jnp.where(own0 | own1, 0.0, rows))
        yield
    done.append(rows)


LAZY = 8


def inverse_half(matrix):
    size = matrix.shape[0]
    count = size // ROWS
    lane = lax.broadcasted_iota(jnp.int32, (ROWS, size), 1)
    groups = [matrix[ROWS * i:ROWS * i + ROWS, :] for i in range(count)]

    def update(i, t, pivots, own):
        rows = groups[i]
        change = rows[:, ROWS * t:ROWS * t + 1] * pivots[0:1, :]
        for j in range(1, ROWS):
            change = change + rows[:, ROWS * t + j:ROWS * t + j + 1] * pivots[j:j + 1, :]
        groups[i] = jnp.where(own, 0.0, rows) - change

    done = []
    for _ in pivot_steps(groups[0], 0, done):
        pass
    groups[0] = done[0]
    for t in range(count):
        pivots = groups[t]
        own = (lane >= ROWS * t) & (lane < ROWS * t + ROWS)
        waiting = list(range(t + 2, count)) + list(range(LAZY * (t // LAZY), t))
        if t + 1 < count:
            update(t + 1, t, pivots, own)
            done = []
            share = -(-len(waiting) // (ROWS // 2 + 1))
            for _ in pivot_steps(groups[t + 1], ROWS * (t + 1), done):
                for i in waiting[:share]:
                    update(i, t, pivots, own)
                waiting = waiting[share:]
            groups[t + 1] = done[0]
        for i in waiting:
            update(i, t, pivots, own)
        if t % LAZY == LAZY - 1 and t >= LAZY:
            start = LAZY * (t // LAZY)
            before = jnp.concatenate(groups[:start], axis=0)
            run = jnp.concatenate(groups[start:start + LAZY], axis=0)
            low, high = ROWS * start, ROWS * (start + LAZY)
            columns = lax.broadcasted_iota(jnp.int32, before.shape, 1)
            kept = jnp.where((columns >= low) & (columns < high), 0.0, before)
            before = kept - dot(before[:, low:high], run)
            for i in range(start):
                groups[i] = before[ROWS * i:ROWS * i + ROWS]
    return jnp.concatenate(groups, axis=0)


def half_indices():
    row = lax.broadcasted_iota(jnp.int32, (HALF, HALF), 0)
    column = lax.broadcasted_iota(jnp.int32, (HALF, HALF), 1)
    return row, column


def pack(matrix, out):
    row, column = half_indices()
    low = matrix[HALF:, HALF:]
    out[:HALF] = matrix[:HALF, HALF:]
    out[HALF:ORB] = jnp.where(row <= column, matrix[:HALF, :HALF], low)
    diagonal = jnp.sum(jnp.where(row == column, low, 0.0), axis=0, keepdims=True)
    out[ORB:] = jnp.broadcast_to(diagonal, (ROWS, HALF))


def unpack_ends(both, diagonal):
    row, column = half_indices()
    turned = both.T
    top = jnp.where(row <= column, both, turned)
    low = jnp.where(row > column, both, turned)
    return top, jnp.where(row == column, diagonal, low)


def unpack(packed):
    corner = packed[:HALF]
    top, low = unpack_ends(packed[HALF:ORB], packed[ORB:ORB + 1])
    return jnp.concatenate(
        [jnp.concatenate([top, corner], axis=1), jnp.concatenate([corner.T, low], axis=1)], axis=0
    )


def message(source, target, send, recv, to, axis="domain"):
    return pltpu.make_async_remote_copy(
        src_ref=source, dst_ref=target, send_sem=send, recv_sem=recv,
        device_id={axis: to}, device_id_type=pl.DeviceIdType.MESH,
    )


def energy_peers():
    me = lax.axis_index("energy")
    count = lax.axis_size("energy")
    core = lax.rem(me, 2)
    return me + 1 - 2 * core, lambda k: lax.rem(me + 2 * k, count)


def energy_part(
    inverse, coulomb, out, green, landed, parity, to_twin, sums_of, from_twin, returned, final,
    own_sem, spread_sem, twin_sem,
):
    me = lax.axis_index("energy")
    chip, core = me // 2, lax.rem(me, 2)
    chips = green.shape[0]
    twin, other = energy_peers()
    first_core = core == 0

    def exchange(source, target, index):
        own = pltpu.make_async_copy(source.at[chip], target.at[chip], own_sem.at[index])
        own.start()

        def send(k, carry):
            to = other(lax.rem(k + chips // 2 - 2, chips - 1) + 1)
            message(
                source.at[to // 2], target.at[chip], spread_sem.at[0, index], spread_sem.at[1, index], to, "energy",
            ).start()
            return carry

        lax.fori_loop(1, chips, send, 0)
        return own, message(
            source.at[pl.ds(0, chips - 1)], target.at[pl.ds(0, chips - 1)],
            spread_sem.at[0, index], spread_sem.at[1, index], other(1), "energy",
        )

    for t in range(chips):
        rows = inverse[ROWS * t:ROWS * t + ROWS, :]
        green[t] = jnp.concatenate([rows[:, :HALF], rows[:, HALF:]], axis=0).astype(jnp.bfloat16)
    own, rest = exchange(green, landed, 0)
    pad = jnp.zeros((2, 4, ROWS, HALF), jnp.float32)
    parity[:, :4] = pad
    parity[:, 4 + chips:] = pad
    factor = jnp.concatenate([coulomb[0, :, :HALF], coulomb[0, :, HALF:]], axis=0)
    factor = factor * factor
    own.wait()
    rest.wait()
    for t in range(chips):
        both = landed[t].astype(jnp.float32)
        upper = jnp.concatenate([both[:4], both[8:12]], axis=0)
        lower = jnp.concatenate([both[4:8], both[12:]], axis=0)
        parity[core, 4 + t] = jnp.where(first_core, upper, lower)
        to_twin[t] = jnp.where(first_core, lower, upper)
    swap = message(to_twin, parity.at[core, pl.ds(4, chips)], twin_sem.at[0], twin_sem.at[1], twin, "energy")
    swap.start()
    swap.wait()

    def at(energy):
        return parity[energy % 2, 4 + energy // 2]

    blocks = 2 * chips // 8
    for kb in range(blocks):
        sums = [None] * 8
        for jb in range(blocks - kb):
            base = [at(8 * jb + a) for a in range(8)]
            ahead = [at(8 * (jb + kb) + c) for c in range(15)]
            for b in range(8):
                for a in range(8):
                    term = base[a] * ahead[a + b]
                    sums[b] = term if sums[b] is None else sums[b] + term
        for b in range(8):
            returned[8 * kb + b] = factor * sums[b]
    for kb in range(blocks):
        sums = [None] * 8
        for jb in range(kb + 1):
            base = [returned[8 * jb + a] for a in range(8)]
            behind = [at(8 * (kb - jb) + c - 7) for c in range(15)]
            for b in range(8):
                for a in range(8):
                    term = base[a] * behind[b - a + 7]
                    sums[b] = term if sums[b] is None else sums[b] + term
        for b in range(8):
            sums_of[b % 2, 4 * kb + b // 2] = sums[b]
    swap = message(sums_of.at[1 - core], from_twin, twin_sem.at[2], twin_sem.at[3], twin, "energy")
    swap.start()
    swap.wait()
    for t in range(chips):
        mine, theirs = sums_of[core, t], from_twin[t]
        upper = jnp.where(first_core, mine, theirs)
        lower = jnp.where(first_core, theirs, mine)
        both = jnp.concatenate([upper[:4], lower[:4], upper[4:], lower[4:]], axis=0)
        green[t] = both.astype(jnp.bfloat16)
    own, rest = exchange(green, final, 1)
    own.wait()
    rest.wait()
    out[...] = final[...]


ENERGY_SCRATCH = (
    ((32, 16, HALF), jnp.bfloat16), ((32, 16, HALF), jnp.bfloat16), ((2, 40, ROWS, HALF), jnp.float32),
    ((32, ROWS, HALF), jnp.float32), ((2, 32, ROWS, HALF), jnp.float32), ((32, ROWS, HALF), jnp.float32),
    ((64, ROWS, HALF), jnp.float32), ((32, 16, HALF), jnp.bfloat16),
)


def energy_scratch():
    return [pltpu.VMEM(*buffer) for buffer in ENERGY_SCRATCH] + [
        pltpu.SemaphoreType.DMA((2,)), pltpu.SemaphoreType.DMA((2, 2)), pltpu.SemaphoreType.DMA((4,)),
    ]


CHUNKS = ((128, 64), (192, 72), (0, 64), (64, 64))
ENDS, CORNER = pl.ds(HALF, PACKED - HALF), pl.ds(0, HALF)


def chain_kernel(
    shift, hamilton, coupling, left_contact, right_contact, coulomb, out,
    block, matrix, inverse, part, part_inverse, solved, lead, side,
    ups, downs, links, toward, away, longer, across,
    to_ring, from_ring, to_pair, from_pair, to_middle, middle, settled, distant, opposite,
    load_sem, send_sem, recv_sem, pair_sem, near_sem, far_sem, middle_sem,
    green, landed, parity, to_twin, sums_of, from_twin, returned, final, own_sem, spread_sem, twin_sem,
):
    place = lax.axis_index("domain")
    count = lax.axis_size("domain")
    chips = green.shape[0]
    twin, other = energy_peers()
    quarter = place // 4
    inner = (place >= 4) & (place < 12)
    odd = lax.rem(quarter, 2)
    even = odd == 0
    pair, near, far = place + 4 - 8 * odd, place + 12 - 8 * quarter, lax.rem(place + 8, count)
    loads = [
        pltpu.make_async_copy(source.at[0], target, load_sem.at[i])
        for i, (source, target) in enumerate(
            ((hamilton, block), (coupling, ups.at[0]), (left_contact, lead), (right_contact, side))
        )
    ]
    for load in loads:
        load.start()

    def neighbour(by):
        return lax.rem(place + by + count, count)

    peers = [neighbour(1), neighbour(-1), neighbour(2), neighbour(-2), pair, near, far]
    barrier = pltpu.get_barrier_semaphore()
    for peer in peers:
        pl.semaphore_signal(barrier, inc=1, device_id={"domain": peer}, device_id_type=pl.DeviceIdType.MESH)

    def greet(k, carry):
        pl.semaphore_signal(barrier, inc=1, device_id={"energy": other(k)}, device_id_type=pl.DeviceIdType.MESH)
        return carry

    lax.fori_loop(1, chips, greet, 0)
    pl.semaphore_signal(barrier, inc=1, device_id={"energy": twin}, device_id_type=pl.DeviceIdType.MESH)
    first_link = message(coupling.at[0], downs.at[0], send_sem.at[0], recv_sem.at[0], neighbour(-1))

    def ring_messages(turn):
        stride = turn + 1
        left, right = neighbour(-stride), neighbour(stride)
        base = 1 + 6 * turn
        return [
            message(
                to_ring.at[turn, side_id, rows], from_ring.at[turn, side_id, rows],
                send_sem.at[base + i], recv_sem.at[base + i], to,
            )
            for i, (side_id, rows, to) in enumerate(
                ((0, ENDS, left), (1, ENDS, right), (0, CORNER, left), (1, CORNER, right))
            )
        ] + [
            message(links.at[turn], downs.at[turn + 1], send_sem.at[base + 4], recv_sem.at[base + 4], left),
            message(links.at[turn], ups.at[turn + 1], send_sem.at[base + 5], recv_sem.at[base + 5], right),
        ]

    def chunk_messages(source, target, send, recv, to):
        return [
            message(source.at[pl.ds(*rows)], target.at[pl.ds(*rows)], send.at[i], recv.at[i], to)
            for i, rows in enumerate(CHUNKS)
        ]

    pair_messages = chunk_messages(to_pair, from_pair, pair_sem.at[0], pair_sem.at[1], pair)
    near_messages = chunk_messages(settled, opposite, near_sem.at[0], near_sem.at[1], near)
    far_messages = chunk_messages(distant, opposite, far_sem.at[0], near_sem.at[1], far)
    middle_messages = chunk_messages(to_middle, middle, middle_sem.at[0], middle_sem.at[1], near)
    link_message = message(longer, across, send_sem.at[13], recv_sem.at[13], pair)

    def before_first():
        for load in loads:
            load.wait()
        row = lax.broadcasted_iota(jnp.int32, (ORB, ORB), 0)
        column = lax.broadcasted_iota(jnp.int32, (ORB, ORB), 1)
        block[...] += jnp.where(row == column, shift[0], 0.0)

        @pl.when(place == 0)
        def _():
            link = ups[0]
            block[...] += dot(link, dot(lead[...], link), 0, 0)
            ups[0] = jnp.zeros((ORB, ORB), jnp.float32)

        @pl.when(place == count - 1)
        def _():
            block[...] += side[...]

        matrix[...] = block[...]

    def before_ring(turn):
        messages = ring_messages(turn)
        messages[0].wait_recv()
        messages[1].wait_recv()

        @pl.when(turn == 0)
        def _():
            messages[2].wait_recv()
            messages[3].wait_recv()
            left_inverse = unpack(from_ring[0, 1])
            block[...] -= dot(ups[0], dot(left_inverse, ups[0]), 0, 0)
            block[...] -= unpack(from_ring[0, 0])
            matrix[...] = block[...]

        @pl.when(turn == 1)
        def _():
            ends = from_ring[1, 0, HALF:, :] + from_ring[1, 1, HALF:, :]
            top, low = unpack_ends(ends[:HALF], ends[HALF:HALF + 1])
            block[:HALF, :HALF] -= top
            block[HALF:, HALF:] -= low
            matrix[:HALF, :HALF] = block[:HALF, :HALF]
            matrix[HALF:, HALF:] = block[HALF:, HALF:]

    def before_ring_corner():
        for received in ring_messages(1)[2:4]:
            received.wait_recv()
        corner = block[:HALF, HALF:] - from_ring[1, 0, :HALF, :] - from_ring[1, 1, :HALF, :]
        block[:HALF, HALF:] = corner
        block[HALF:, :HALF] = corner.T
        matrix[:HALF, HALF:] = corner

    def before_middle():
        @pl.when(inner)
        def _():
            pack(block[...], settled)
            for i, rows in enumerate(CHUNKS):
                pair_messages[i].wait_recv()
                settled[pl.ds(*rows)] -= from_pair[pl.ds(*rows)]
                near_messages[i].start()
                middle_messages[i].wait_recv()
                distant[pl.ds(*rows)] = settled[pl.ds(*rows)] - middle[pl.ds(*rows)]
                far_messages[i].start()
            block[...] = unpack(settled[...])
            for received in near_messages[:2]:
                received.wait_recv()

        @pl.when(jnp.logical_not(inner))
        def _():
            for received in pair_messages:
                received.wait_recv()
            block[...] -= unpack(from_pair[...])
            for received in far_messages[:2]:
                received.wait_recv()

        ends = opposite[HALF:, :]
        top, low = unpack_ends(ends[:HALF], ends[HALF:HALF + 1])
        matrix[:HALF, :HALF] = top
        matrix[HALF:, HALF:] = low

    def before_middle_corner():
        for received in near_messages[2:]:
            received.wait_recv()
        matrix[:HALF, HALF:] = opposite[:HALF, :]

    def before_last():
        @pl.when(inner)
        def _():
            across[...] = away[...].T

        @pl.when(jnp.logical_not(inner))
        def _():
            link_message.wait_recv()

        link = across[...]
        block[...] -= dot(link, dot(inverse[...], link), 0, 0)
        matrix[...] = block[...]

    def after_ring(turn):
        messages = ring_messages(turn)

        @pl.when(turn == 0)
        def _():
            pack(inverse[...], to_ring.at[turn, 1])
            messages[1].start()
            messages[3].start()

        @pl.when(turn == 1)
        def _():
            for received in ring_messages(0)[4:]:
                received.wait_recv()

        pack(dot(ups[turn], dot(inverse[...], ups[turn], 1, 1)), to_ring.at[turn, 0])
        messages[0].start()
        messages[2].start()

        @pl.when(turn == 0)
        def _():
            first_link.wait_recv()

            @pl.when(place == count - 1)
            def _():
                downs[0] = jnp.zeros((ORB, ORB), jnp.float32)

        matrix[...] = dot(inverse[...], downs[turn])

        @pl.when(turn == 1)
        def _():
            pack(dot(downs[turn], matrix[...], 0, 0), to_ring.at[turn, 1])
            messages[1].start()
            messages[3].start()

        links[turn] = -dot(ups[turn], matrix[...])
        messages[4].start()
        messages[5].start()

    def after_pair():
        for received in ring_messages(1)[4:]:
            received.wait_recv()
        turned = ups[2].T
        toward[...] = jnp.where(even, downs[2], turned)

        @pl.when(inner)
        def _():
            away[...] = jnp.where(even, turned, downs[2])
            matrix[...] = dot(inverse[...], away[...])
            pack(dot(away[...], matrix[...], 0, 0), to_middle)
            for sent in middle_messages:
                sent.start()

        pack(dot(toward[...], dot(inverse[...], toward[...]), 0, 0), to_pair)
        for sent in pair_messages:
            sent.start()

        @pl.when(inner)
        def _():
            longer[...] = -dot(matrix[...], toward[...], 0, 0)
            link_message.start()

    def turn_half(step, carry):
        turn, half = step // 2, lax.rem(step, 2)

        @pl.when(step == 1)
        def _():
            pl.semaphore_wait(barrier, len(peers) + chips)
            first_link.start()

        @pl.when(half == 0)
        def _():
            pl.when(turn == 0)(before_first)
            pl.when((turn == 1) | (turn == 2))(lambda: before_ring(turn - 1))
            pl.when(turn == 3)(before_middle)
            pl.when(turn == 4)(before_last)
            part[...] = matrix[:HALF, :HALF]

        @pl.when(half == 1)
        def _():
            pl.when(turn == 2)(before_ring_corner)
            pl.when(turn == 3)(before_middle_corner)
            top = part_inverse[...]
            corner = matrix[:HALF, HALF:]
            inverse[:HALF, :HALF] = top
            solved[...] = dot(top, corner)
            part[...] = matrix[HALF:, HALF:] - dot(corner, solved[...], 0, 0)

        part_inverse[...] = inverse_half(part[...])

        @pl.when(half == 1)
        def _():
            low = part_inverse[...]
            corner = dot(solved[...], low)
            inverse[:HALF, :HALF] += dot(corner, solved[...], 1, 1)
            inverse[:HALF, HALF:] = -corner
            inverse[HALF:, :HALF] = -corner.T
            inverse[HALF:, HALF:] = low
            pl.when(turn <= 1)(lambda: after_ring(turn))
            pl.when(turn == 2)(after_pair)

        return carry

    lax.fori_loop(0, 10, turn_half, 0)
    energy_part(
        inverse, coulomb, out, green, landed, parity, to_twin, sums_of, from_twin, returned, final,
        own_sem, spread_sem, twin_sem,
    )
    first_link.wait_send()
    for turn in range(2):
        for sent in ring_messages(turn):
            sent.wait_send()
    for sent in pair_messages:
        sent.wait_send()

    @pl.when(inner)
    def _():
        for sent in (link_message, *middle_messages, *near_messages, *far_messages):
            sent.wait_send()


def on_device(hamilton, coupling, left_contact, right_contact, shifts, coulomb):
    def several(*shape):
        return pltpu.VMEM(shape, jnp.float32)

    square = several(ORB, ORB)
    half = several(HALF, HALF)
    packed = several(PACKED, HALF)
    chunked = pltpu.SemaphoreType.DMA((2, len(CHUNKS)))
    result = pl.pallas_call(
        chain_kernel,
        out_shape=jax.ShapeDtypeStruct((ORB // ROWS, 2 * ROWS, HALF), jnp.bfloat16),
        in_specs=[SMEM] + [pl.BlockSpec(memory_space=pl.ANY)] * 4 + [VMEM],
        out_specs=VMEM,
        scratch_shapes=[
            square, square, square, half, half, half, square, square,
            several(3, ORB, ORB), several(3, ORB, ORB), several(2, ORB, ORB), square, square, square, square,
            several(2, 2, PACKED, HALF), several(2, 2, PACKED, HALF),
            packed, packed, packed, packed, packed, packed, packed,
            pltpu.SemaphoreType.DMA((4,)), pltpu.SemaphoreType.DMA((14,)), pltpu.SemaphoreType.DMA((14,)),
            chunked, chunked, chunked, chunked, *energy_scratch(),
        ],
        compiler_params=pltpu.CompilerParams(
            vmem_limit_bytes=56 * 1024 * 1024, collective_id=0, has_side_effects=True,
        ),
    )(shifts, hamilton, coupling, left_contact, right_contact, coulomb)
    result = result.reshape(ORB // ROWS, 2, ROWS, HALF).transpose(0, 2, 1, 3)
    return result.reshape(1, 1, ORB, ORB)


def solution(mesh):
    placed = (
        P("domain", None, None),
        P("domain", None, None),
        P("energy", None, None),
        P("energy", None, None),
        P("energy"),
        P("domain", "energy", None),
    )
    return jax.shard_map(
        on_device,
        mesh=mesh,
        in_specs=placed,
        out_specs=P("energy", "domain", None, None),
        check_vma=False,
    )
```
